256 devices in a mesh: enc: 32 (over y, z), dec: 4 (over x), mdl: 2 (over core).
Axes of the slice: x: 4, y: 4, z: 8, core: 2. Of those that a mesh axis runs over, the one named last changes fastest.
Arguments:
- passages: bfloat16 [384, 256, 4096], P(('enc', 'dec')), may hold values from -6 to 6
- norm_gain: bfloat16 [4096], replicated, may hold values from 0.099609375 to 1.8984375
- w_key: bfloat16 [4096, 2048], P(('enc', 'dec'), 'mdl'), may hold values from -0.09375 to 0.09375
- w_value: bfloat16 [4096, 2048], P(('enc', 'dec'), 'mdl'), may hold values from -0.375 to 0.375
- queries: bfloat16 [64, 64, 2048], P('enc', None, 'mdl'), may hold values from -18 to 18
- lengths: int32 [384], P(('enc', 'dec')), may hold values from 1 to 256
- passage_question: int32 [384], P(('enc', 'dec')), may hold values from 0 to 63, as said below
Outputs:
- context: bfloat16 [64, 64, 2048], P('enc', None, 'mdl')
The draws below stay inside these ranges and needn't reach their ends.
Inputs may be any that keep to these rules, and one draw needn't show every extreme that they name: Passage p serves a question of its own group: p // 12 * 2 <= passage_question[p] < (p // 12 + 1) * 2, and every question has at least one passage.
All inputs are finite; a program needn't handle non-finite values.
Results may differ from the reference program's by a relative error of at most 0.009.
The reference program's roundings to bfloat16 on the way (of `normed`, `key_rows`, `value_rows` and `weights`) count: a program that leaves them out, or rounds other values in their place, can miss the bound.
Values may be sent and summed in bfloat16 or wider, within the bound.
No kernel may reach another device: no remote copies, remote signals or barrier semaphores. Data moves between devices by JAX's collectives and lax.ppermute only.
A program may use at most 128 MiB of HBM per device.

```python
import jax
import jax.numpy as jnp
from jax import lax

D = 4096
HEADS = 32
HD = 64
L = 256
A = 64
Q_DEV = 2
ROW_PASS = 12
NPASS = 384
Q = 64


def draw_queries(key, part):
    key = jax.random.fold_in(key, 5)
    first = jax.random.fold_in(key, 0)
    shape = (Q, A, HEADS * HD)
    values = jnp.clip(jax.random.normal(first, shape, jnp.float32) * 0.25, -1.5, 1.5)
    return values.astype(jnp.bfloat16)


def draw_passage_question(key, part):
    key = jax.random.fold_in(key, 11)
    groups = NPASS // ROW_PASS
    first, second, third = jax.random.split(key, 3)
    pick = jnp.minimum(jax.random.randint(first, (groups, ROW_PASS), 0, Q_DEV), jax.random.randint(second, (groups, ROW_PASS), 0, Q_DEV))
    order = jax.vmap(lambda sub: jax.random.permutation(sub, ROW_PASS))(jax.random.split(third, groups))
    ranking = jnp.argsort(order, axis=1, stable=True).astype(jnp.int32)
    pick = jnp.where(ranking < Q_DEV, ranking, pick)
    owner = pick + jnp.arange(groups, dtype=jnp.int32)[:, None] * Q_DEV
    return owner.reshape(NPASS).astype(jnp.int32)


def touch_ends(values, rng, least, top_value):
    longest = values.shape.index(max(values.shape))
    spots = []
    for shift in (0, 1):
        where = [jax.random.randint(jax.random.fold_in(rng, axis), (), 0, length) for axis, length in enumerate(values.shape)]
        where[longest] = (where[longest] + shift) % values.shape[longest]
        spots.append(tuple(where))
    return values.at[spots[0]].set(least).at[spots[1]].set(top_value)


def with_spikes(entries, rng, source, target, blocks, factor):
    owner, partner = [(jnp.arange(entries.shape[dim]) // (entries.shape[dim] // blocks)).reshape([-1 if axis == dim else 1 for axis in range(entries.ndim)]) for dim in (source, target)]
    chosen = jax.random.permutation(rng, blocks)[partner]
    strong = (owner == chosen) | (owner == (partner + blocks // 2) % blocks)
    return jnp.where(strong, factor * entries, entries)


def block_scale(stream_key, extent, cuts, low, largest):
    gain, own = 1.0, jax.random.fold_in(stream_key, 6)
    for axis_at, shards_of in cuts:
        draws = jnp.exp(jax.random.uniform(jax.random.fold_in(own, axis_at), (shards_of,), jnp.float32, low / len(cuts), largest / len(cuts)))
        gain = gain * jnp.repeat(draws, extent[axis_at] // shards_of).reshape([-1 if axis == axis_at else 1 for axis in range(len(extent))])
    return gain


def centred(own_key, shape, deviation, most, cuts=(), held_as=jnp.bfloat16):
    loudness = block_scale(own_key, shape, cuts, -0.22, 0.18) if cuts else 1.0
    drawn = jax.random.normal(own_key, shape, jnp.float32) * deviation * loudness
    return jnp.minimum(jnp.maximum(drawn, -most), most).astype(held_as)


def gaussian_with(rng, shape, spread, bound, pieces, heavy, held_as=jnp.bfloat16):
    values = spread * jax.random.normal(rng, shape, jnp.float32)
    if pieces:
        values = values * block_scale(rng, shape, pieces, -0.22, 0.18)
    return jnp.clip(with_spikes(values, jax.random.fold_in(rng, 3), *heavy), -bound, bound).astype(held_as)


def setup_inputs(seed: int = 0) -> dict:
    arg_keys = jax.random.split(jax.random.key(seed), 8)
    passages = centred(arg_keys[0], (NPASS, L, D), 1.0, 6.0, ((0, 128),))
    norm_gain = jnp.clip(1.0 + 0.18 * jax.random.normal(arg_keys[1], (D,), jnp.float32), 0.099609375, 1.8984375).astype(jnp.bfloat16)
    w_key = centred(arg_keys[2], (D, HEADS * HD), D ** -0.5, 0.09375, ((0, 128), (1, 2)))
    w_value = gaussian_with(arg_keys[3], (D, HEADS * HD), D ** -0.5, 0.375, ((0, 128), (1, 2)), (0, 1, 128, 5.5))
    queries = draw_queries(jax.random.fold_in(arg_keys[7], 71), 0)
    lengths = touch_ends(jax.random.randint(arg_keys[5], (NPASS,), 1, L + 1), jax.random.fold_in(arg_keys[5], 1), 1, L).astype(jnp.int32)
    passage_question = draw_passage_question(jax.random.fold_in(arg_keys[7], 71), 0)
    return dict(passages=passages, norm_gain=norm_gain, w_key=w_key, w_value=w_value, queries=queries, lengths=lengths, passage_question=passage_question)


def encode(group_pass, norm_gain, w_key, w_value):
    states = group_pass.astype(jnp.float32)
    scale = lax.rsqrt(lax.optimization_barrier(jnp.mean(states * states, axis=-1, keepdims=True)) + 1e-06)
    normed = (states * scale * norm_gain.astype(jnp.float32)).astype(jnp.bfloat16)
    flat = normed.reshape(-1, D)
    key_rows = jnp.dot(flat, w_key, preferred_element_type=jnp.float32).astype(jnp.bfloat16)
    value_rows = jnp.dot(flat, w_value, preferred_element_type=jnp.float32).astype(jnp.bfloat16)
    return (key_rows, value_rows)

def reference(passages, norm_gain, w_key, w_value, queries, lengths, passage_question):
    groups = NPASS // ROW_PASS
    group_states = passages.reshape(groups, ROW_PASS, L, D)
    group_queries = queries.reshape(groups, Q_DEV * A, HEADS, HD)
    group_lengths = lengths.reshape(groups, ROW_PASS)
    group_owner = passage_question.reshape(groups, ROW_PASS)
    group_index = jnp.arange(groups, dtype=jnp.int32)

    def one_group(items):
        states, query_rows, lens, owner, index = items
        key_rows, value_rows = encode(states, norm_gain, w_key, w_value)
        key_heads = key_rows.reshape(-1, HEADS, HD).astype(jnp.float32)
        value_heads = value_rows.reshape(-1, HEADS, HD).astype(jnp.float32)
        scores = jnp.einsum('rhc,khc->hrk', query_rows.astype(jnp.float32), key_heads)
        row_question = index * Q_DEV + jnp.arange(Q_DEV * A, dtype=jnp.int32) // A
        key_question = jnp.repeat(owner, L)
        slot = jnp.arange(ROW_PASS * L, dtype=jnp.int32) % L
        key_live = slot < jnp.repeat(lens, L)
        allowed = (row_question[:, None] == key_question[None, :]) & key_live[None, :]
        masked = jnp.where(allowed[None], scores, -1e+30)
        row_max = lax.optimization_barrier(jnp.max(masked, axis=2))
        weights = jnp.where(allowed[None], jnp.exp(masked - row_max[..., None]), 0.0)
        denominator = lax.optimization_barrier(jnp.sum(weights, axis=2))
        rounded = weights.astype(jnp.bfloat16).astype(jnp.float32)
        numerator = jnp.einsum('hrk,khc->hrc', rounded, value_heads)
        result = numerator / denominator[..., None]
        return jnp.transpose(result, (1, 0, 2)).reshape(Q_DEV, A, HEADS * HD).astype(jnp.bfloat16)
    outcome = lax.map(one_group, (group_states, group_queries, group_lengths, group_owner, group_index))
    return outcome.reshape(Q, A, HEADS * HD)
```

```python
import functools

import jax
import jax.numpy as jnp
from jax import lax
from jax.experimental import pallas as pl
from jax.experimental.pallas import tpu as pltpu
from jax.sharding import PartitionSpec as P

HD = 64
NY, NZ, NX, NC = 4, 8, 4, 2
DY = (0, -1, 1, 2)
DZ = (0, -1, -2, -3, 1, 2, 3, 4)
VMEM_LIMIT = 56 * 1024 * 1024
NEG = -1e30
TILE = 384
UNIT = 128


def shift_z(value, step):
    pairs = [(y * NZ + z, y * NZ + (z + step) % NZ) for y in range(NY) for z in range(NZ)]
    return lax.ppermute(value, "enc", pairs)


def shift_y(value, step):
    pairs = [(y * NZ + z, (y + step) % NY * NZ + z) for y in range(NY) for z in range(NZ)]
    return lax.ppermute(value, "enc", pairs)


def shift_x(value, step):
    return lax.ppermute(value, "dec", [(x, (x + step) % NX) for x in range(NX)])


def split_x(value):
    pairs = [
        (x * NC + c, (x + (1 if c == 0 else -1)) % NX * NC + c) for x in range(NX) for c in range(NC)
    ]
    return lax.ppermute(value, ("dec", "mdl"), pairs)


def other_core(value):
    return lax.ppermute(value, "mdl", [(0, 1), (1, 0)])


def norm_kernel(order_ref, x_ref, gain_ref, o_ref):
    states = x_ref[...].astype(jnp.float32)
    width = states.shape[1]
    scale = lax.rsqrt(jnp.sum(states * states, axis=1, keepdims=True) * (1.0 / width) + 1e-06)
    for k in range(width // 128):
        start = pl.multiple_of(order_ref[k] * 128, 128)
        part = x_ref[:, pl.ds(start, 128)].astype(jnp.float32)
        gain = gain_ref[:, pl.ds(start, 128)].astype(jnp.float32)
        o_ref[:, k * 128 : (k + 1) * 128] = (part * scale * gain).astype(jnp.bfloat16)


def normalise(order, states, gain):
    rows, width = states.shape
    return pl.pallas_call(
        norm_kernel,
        out_shape=jax.ShapeDtypeStruct((rows, width), jnp.bfloat16),
        grid_spec=pltpu.PrefetchScalarGridSpec(
            num_scalar_prefetch=1,
            grid=(rows // UNIT,),
            in_specs=[
                pl.BlockSpec((UNIT, width), lambda i, order: (i, 0)),
                pl.BlockSpec((1, width), lambda i, order: (0, 0)),
            ],
            out_specs=pl.BlockSpec((UNIT, width), lambda i, order: (i, 0)),
        ),
        compiler_params=pltpu.CompilerParams(vmem_limit_bytes=VMEM_LIMIT),
        cost_estimate=pl.CostEstimate(
            flops=6 * rows * width, bytes_accessed=4 * rows * width, transcendentals=rows
        ),
    )(order, states, gain)


def value_columns(x, j):
    return jnp.concatenate(
        [x[:, i * 1024 + j * 128 : i * 1024 + (j + 1) * 128] for i in range(NY)], axis=1
    )


def project_kernel(own_ref, near_ref, far_ref, *refs):
    key_refs, value_refs = refs[:3], refs[3:10]
    key_out, value_out, rest_out = refs[10:]
    step = pl.program_id(0)

    def run(x_ref):
        total = None
        for i, w_ref in enumerate(key_refs):
            part = jnp.dot(
                x_ref[:, i * 1024 : (i + 1) * 1024], w_ref[...], preferred_element_type=jnp.float32
            )
            total = part if total is None else total + part
        key_out[...] = total
        total = None
        for j, w_ref in enumerate(value_refs):
            part = jnp.dot(
                value_columns(x_ref, j), w_ref[...], preferred_element_type=jnp.float32
            )
            total = part if total is None else total + part
        value_out[...] = total
        rest_out[:, :1024] = x_ref[:, 3072:4096]
        rest_out[:, 1024:] = value_columns(x_ref, 7)

    pl.when(step < 2)(lambda: run(own_ref))
    pl.when(step == 2)(lambda: run(near_ref))
    pl.when(step == 3)(lambda: run(far_ref))


def project(own, near, far, key_parts, value_parts):
    rows = own.shape[0] + near.shape[0] + far.shape[0]
    width, cols = own.shape[1], key_parts[0].shape[1]
    steps = rows // TILE
    whole = lambda a: pl.BlockSpec(a.shape, lambda i: (0, 0))
    return pl.pallas_call(
        project_kernel,
        out_shape=(
            jax.ShapeDtypeStruct((rows, cols), jnp.float32),
            jax.ShapeDtypeStruct((rows, cols), jnp.float32),
            jax.ShapeDtypeStruct((rows, 1536), jnp.bfloat16),
        ),
        grid=(steps,),
        in_specs=[
            pl.BlockSpec((TILE, width), lambda i: (jnp.minimum(i, 1), 0)),
            whole(near),
            whole(far),
        ]
        + [whole(a) for a in key_parts]
        + [whole(a) for a in value_parts],
        out_specs=(
            pl.BlockSpec((TILE, cols), lambda i: (i, 0)),
            pl.BlockSpec((TILE, cols), lambda i: (i, 0)),
            pl.BlockSpec((TILE, 1536), lambda i: (i, 0)),
        ),
        compiler_params=pltpu.CompilerParams(vmem_limit_bytes=VMEM_LIMIT),
        cost_estimate=pl.CostEstimate(
            flops=2 * rows * cols * (3072 + 3584),
            bytes_accessed=rows * width * 2 + 6656 * cols * 2 + rows * cols * 8,
            transcendentals=0,
        ),
    )(own, near, far, *key_parts, *value_parts)


def split3(x):
    high = x.astype(jnp.bfloat16)
    rest = x - high.astype(jnp.float32)
    mid = rest.astype(jnp.bfloat16)
    low = (rest - mid.astype(jnp.float32)).astype(jnp.bfloat16)
    return [high, mid, low]


def attend_kernel(
    owner_ref, live_ref, key_acc, value_acc, rest_ref, wk0, wk1, wv0, wv1, q_ref, o_ref, num, top, tot
):
    step = pl.program_id(0)

    @pl.when(step == 0)
    def _():
        num[...] = jnp.zeros_like(num)
        tot[...] = jnp.zeros_like(tot)
        top[...] = jnp.full_like(top, NEG)

    def dot(a, b):
        return jnp.dot(a, b, preferred_element_type=jnp.float32)

    keys = key_acc[...] + dot(rest_ref[:, :512], wk0[...]) + dot(rest_ref[:, 512:1024], wk1[...])
    keys = keys.astype(jnp.bfloat16)
    values = (
        value_acc[...] + dot(rest_ref[:, 1024:1280], wv0[...]) + dot(rest_ref[:, 1280:], wv1[...])
    )
    values = values.astype(jnp.bfloat16)
    slot = lax.broadcasted_iota(jnp.int32, (UNIT, 256), 0)
    for u in range(TILE // UNIT):
        unit = step * (TILE // UNIT) + u
        valid = slot < live_ref[unit]
        for g in range(2):
            at = owner_ref[unit] * 2 + g
            part = (slice(u * UNIT, (u + 1) * UNIT), slice(g * 256, (g + 1) * 256))
            scores = jnp.where(valid, dot(keys[part], q_ref[at]), NEG)
            old = top[at, 0:1, :]
            new = jnp.maximum(old, jnp.max(scores, axis=0, keepdims=True))
            fade = jnp.exp(old - new)
            weights = jnp.where(valid, jnp.exp(scores - new), 0.0)
            top[at, 0:1, :] = new
            tot[at, 0:1, :] = tot[at, 0:1, :] * fade + jnp.sum(weights, axis=0, keepdims=True)
            added = lax.dot_general(
                values[part],
                weights.astype(jnp.bfloat16),
                (((0,), (0,)), ((), ())),
                preferred_element_type=jnp.float32,
            )
            num[at] = num[at] * fade + added

    @pl.when(step == pl.num_programs(0) - 1)
    def _():
        for head in range(8):
            g, a = head // 4, head % 4 * HD
            join = lambda ref, r0, r1: jnp.concatenate(
                [ref[q * 2 + g, r0:r1, a : a + HD] for q in range(2)], axis=1
            )
            o_ref[head, :HD, :] = join(num, a, a + HD).astype(jnp.bfloat16)
            lines = split3(join(top, 0, 1)) + split3(join(tot, 0, 1))
            lines.append(jnp.zeros((10, 128), jnp.bfloat16))
            o_ref[head, HD:, :] = jnp.concatenate(lines, axis=0)


def attend(owner, live, key_acc, value_acc, rest, key_last, value_last, query_blocks):
    rows, cols = key_acc.shape
    whole = lambda a: pl.BlockSpec(a.shape, lambda i, *_: (0,) * a.ndim)
    tiled = lambda a: pl.BlockSpec((TILE, a.shape[1]), lambda i, *_: (i, 0))
    ends = list(key_last) + list(value_last)
    return pl.pallas_call(
        attend_kernel,
        out_shape=jax.ShapeDtypeStruct((8, 80, 128), jnp.bfloat16),
        grid_spec=pltpu.PrefetchScalarGridSpec(
            num_scalar_prefetch=2,
            grid=(rows // TILE,),
            in_specs=[tiled(key_acc), tiled(value_acc), tiled(rest)]
            + [whole(a) for a in ends]
            + [whole(query_blocks)],
            out_specs=pl.BlockSpec((8, 80, 128), lambda i, *_: (0, 0, 0)),
            scratch_shapes=[
                pltpu.VMEM((4, 256, 256), jnp.float32),
                pltpu.VMEM((4, 8, 256), jnp.float32),
                pltpu.VMEM((4, 8, 256), jnp.float32),
            ],
        ),
        compiler_params=pltpu.CompilerParams(vmem_limit_bytes=VMEM_LIMIT),
        cost_estimate=pl.CostEstimate(
            flops=2 * rows * cols * (1536 + 1024),
            bytes_accessed=rows * cols * 8 + rows * 1536 * 2 + 1536 * cols * 2,
            transcendentals=rows * 512,
        ),
    )(owner, live, key_acc, value_acc, rest, *ends, query_blocks)


def combine_kernel(colour_ref, own, opposite, left, right, o_ref):
    def exact(ref, head, row):
        part = lambda r: ref[head, r : r + 1, :].astype(jnp.float32)
        return part(row) + part(row + 1) + part(row + 2)

    def head_result(a, b, head):
        top_a, top_b = exact(a, head, HD), exact(b, head, HD)
        top = jnp.maximum(top_a, top_b)
        fade_a, fade_b = jnp.exp(top_a - top), jnp.exp(top_b - top)
        total = exact(a, head, HD + 3) * fade_a + exact(b, head, HD + 3) * fade_b
        sums = a[head, :HD, :].astype(jnp.float32) * fade_a
        sums = sums + b[head, :HD, :].astype(jnp.float32) * fade_b
        return sums / total

    for side, (a, b) in enumerate(((own, opposite), (left, right))):
        colour = colour_ref[0] if side == 0 else 1 - colour_ref[0]
        for pair in range(4):
            block = jnp.concatenate(
                [head_result(a, b, 2 * pair), head_result(a, b, 2 * pair + 1)], axis=0
            )
            start = pl.multiple_of(colour * 512 + pair * 128, 128)
            o_ref[:, pl.ds(start, 128)] = block.T.astype(jnp.bfloat16)


def combine(colour, own, opposite, left, right):
    return pl.pallas_call(
        combine_kernel,
        out_shape=jax.ShapeDtypeStruct((128, 1024), jnp.bfloat16),
        in_specs=[pl.BlockSpec(memory_space=pltpu.SMEM)]
        + [pl.BlockSpec(memory_space=pltpu.VMEM)] * 4,
        out_specs=pl.BlockSpec(memory_space=pltpu.VMEM),
        compiler_params=pltpu.CompilerParams(vmem_limit_bytes=VMEM_LIMIT),
        cost_estimate=pl.CostEstimate(flops=1 << 20, bytes_accessed=1 << 20, transcendentals=4096),
    )(colour, own, opposite, left, right)


def half(matrix, colour):
    return lax.dynamic_slice_in_dim(matrix, colour * 512, 512, axis=1)


def body(passages, norm_gain, w_key, w_value, queries, lengths, passage_question):
    cat = lambda parts: jnp.concatenate(parts, axis=0)
    enc, x, core = lax.axis_index("enc"), lax.axis_index("dec"), lax.axis_index("mdl")
    y, z = enc // NZ, enc % NZ
    colour = x % 2
    pass_local, slot_count, width = passages.shape
    token_count = pass_local * slot_count

    mine = jnp.concatenate([half(w_key, colour), half(w_value, colour)], axis=1)
    theirs = jnp.concatenate([half(w_key, 1 - colour), half(w_value, 1 - colour)], axis=1)
    ring = [mine, shift_x(theirs, -1), shift_x(mine, 2), shift_x(theirs, 1)]
    rows = lax.dynamic_slice_in_dim(cat(ring + ring[:3]), (NX - x) % NX * 32, 128, axis=0)

    order = jnp.stack([(y + dy) % NY * NZ + (z + dz) % NZ for dy in DY for dz in DZ]).astype(jnp.int32)
    own = normalise(order, passages.reshape(token_count, width), norm_gain.reshape(1, width))
    outgoing = lax.dynamic_slice_in_dim(own, core * TILE, TILE, axis=0)
    rows, outgoing = lax.optimization_barrier((rows, outgoing))
    near = split_x(outgoing)

    value_rows, key_rows = rows[:, 512:], rows[:, :512]
    v0 = cat([value_rows, shift_y(value_rows, 1), shift_y(value_rows, -1), shift_y(value_rows, 2)])
    vr1, vl1 = shift_z(v0, 1), shift_z(v0, -1)
    kr1, kl1 = shift_z(key_rows, 1), shift_z(key_rows, -1)
    kr2, kl2 = shift_z(kr1, 1), shift_z(kl1, -1)
    kr3, kl3 = shift_z(kr2, 1), shift_z(kl2, -1)
    kr4, kl4 = shift_z(kr3[:64], 1), shift_z(kl3[64:], -1)
    k0 = cat([key_rows, kr1, kr2, kr3, kl1, kl2, kl3, kr4, kl4])
    vr2, vl2 = shift_z(vr1, 1), shift_z(vl1, -1)
    ky1, ky3 = shift_y(k0, 1), shift_y(k0, -1)
    vr3, vl3 = shift_z(vr2, 1), shift_z(vl2, -1)
    vr4, vl4 = shift_z(vr3[:256], 1), shift_z(vl3[256:], -1)
    ky2a, ky2b = shift_y(ky1[:512], 1), shift_y(ky3[512:], -1)

    near_late, _ = lax.optimization_barrier((near, kr4))
    far = other_core(near_late)

    facts = jnp.concatenate([lengths, passage_question - enc * 2]).reshape(1, 6)
    facts, _ = lax.optimization_barrier((facts, kr1))
    low, high = shift_x(facts, 1)[0], shift_x(facts, -1)[0]
    facts = facts[0]

    def units(facts, chosen):
        live = jnp.stack([facts[p] - at for p, at in chosen])
        return live, jnp.stack([facts[3 + p] for p, _ in chosen])

    every = [(p, at) for p in range(3) for at in (0, 128)]
    own_live, own_owner = units(facts, every)
    low_live, low_owner = units(low, every[:3])
    high_live, high_owner = units(high, every[3:])
    flip = lambda a, b: jnp.where(core == 0, jnp.concatenate([a, b]), jnp.concatenate([b, a]))
    live = jnp.concatenate([own_live, flip(low_live, high_live)]).astype(jnp.int32)
    owner = jnp.concatenate([own_owner, flip(low_owner, high_owner)]).astype(jnp.int32)

    rows_q = half(queries.reshape(128, -1), colour).reshape(2, 64, 2, 4, HD)
    turned = jnp.transpose(rows_q, (0, 2, 3, 4, 1))
    eye = jnp.eye(4, dtype=jnp.bool_)[None, None, :, None, :, None]
    blocks = jnp.where(eye, turned[:, :, :, :, None, :], jnp.zeros((), jnp.bfloat16))
    blocks = blocks.reshape(4, 256, 256)

    key_acc, value_acc, rest = project(
        own, near_late, far, (k0, ky1, ky3), (v0, vr1, vr2, vr3, vl1, vl2, vl3)
    )
    part = attend(owner, live, key_acc, value_acc, rest, (ky2a, ky2b), (vr4, vl4), blocks)
    result = combine(
        colour.reshape(1).astype(jnp.int32),
        part,
        shift_x(part, 2),
        shift_x(part, 1),
        shift_x(part, -1),
    )
    return result.reshape(2, 64, 1024)


def solution(mesh):
    return jax.shard_map(
        body,
        mesh=mesh,
        in_specs=(
            P(("enc", "dec"), None, None),
            P(),
            P(("enc", "dec"), "mdl"),
            P(("enc", "dec"), "mdl"),
            P("enc", None, "mdl"),
            P(("enc", "dec")),
            P(("enc", "dec")),
        ),
        out_specs=P("enc", None, "mdl"),
        check_vma=False,
    )
```

```python
import functools

import jax
import jax.numpy as jnp
from jax import lax
from jax.experimental import pallas as pl
from jax.experimental.pallas import tpu as pltpu
from jax.sharding import PartitionSpec as P

HD = 64
NY, NZ, NX, NC = 4, 8, 4, 2
DY = (0, -1, 1, 2)
DZ = (0, -1, 1, -2, 2, -3, 3, 4)
VMEM_LIMIT = 48 * 1024 * 1024
SMALL_VMEM = 16 * 1024 * 1024
NEG = -1e30
FLOOR = -1e29
TILE = 384
UNIT = 128


def shift_z(value, step):
    pairs = [(y * NZ + z, y * NZ + (z + step) % NZ) for y in range(NY) for z in range(NZ)]
    return lax.ppermute(value, "enc", pairs)


def shift_y(value, step):
    pairs = [(y * NZ + z, (y + step) % NY * NZ + z) for y in range(NY) for z in range(NZ)]
    return lax.ppermute(value, "enc", pairs)


def shift_x(value, step):
    return lax.ppermute(value, "dec", [(x, (x + step) % NX) for x in range(NX)])


def split_x(value):
    pairs = [
        (x * NC + c, (x + (1 if c == 0 else -1)) % NX * NC + c) for x in range(NX) for c in range(NC)
    ]
    return lax.ppermute(value, ("dec", "mdl"), pairs)


def other_core(value):
    return lax.ppermute(value, "mdl", [(0, 1), (1, 0)])


def pick_kernel(colour_ref, key_ref, value_ref, mine_ref, theirs_ref):
    for out, colour in ((mine_ref, colour_ref[0]), (theirs_ref, 1 - colour_ref[0])):
        at = pl.ds(pl.multiple_of(colour * 512, 512), 512)
        out[:, :512] = key_ref[:, at]
        out[:, 512:] = value_ref[:, at]


def place_kernel(x_ref, *refs):
    parts, (key_out, value_out) = refs[:4], refs[4:]
    for j, part in enumerate(parts):
        at = pl.ds(pl.multiple_of((x_ref[0] + j) % NX * 32, 32), 32)
        key_out[at, :] = part[:, :512]
        value_out[at, :] = part[:, 512:]


def whole_block(a):
    return pl.BlockSpec(a.shape, lambda i: (0,) * len(a.shape))


def small_call(kernel, out_shape, scalar, *arrays):
    specs, operands = [whole_block(a) for a in arrays], arrays
    if scalar is not None:
        specs, operands = [pl.BlockSpec(memory_space=pltpu.SMEM)] + specs, (scalar,) + arrays
    return pl.pallas_call(
        kernel,
        out_shape=out_shape,
        grid=(1,),
        in_specs=specs,
        out_specs=jax.tree.map(whole_block, out_shape),
        compiler_params=pltpu.CompilerParams(vmem_limit_bytes=SMALL_VMEM),
        cost_estimate=pl.CostEstimate(
            flops=0, bytes_accessed=4 * sum(a.size for a in arrays), transcendentals=0
        ),
    )(*operands)


def gather_kernel(k0, kr1, kl1, kr2, kl2, v0, vy1, vy3, vy2, right_ref, left_ref, group_ref):
    for j, ref in enumerate((kr2, v0, vy1, vy3, vy2)):
        right_ref[j * 128 : (j + 1) * 128, :] = ref[...]
    for j, ref in enumerate((v0, vy1, vy3, vy2, kl2)):
        left_ref[j * 128 : (j + 1) * 128, :] = ref[...]
    for j, ref in enumerate((k0, kr1, kl1, kr2, kl2)):
        group_ref[j * 128 : (j + 1) * 128, :] = ref[...]


def end_kernel(right, left, ahead, group_ref):
    group_ref[:128, :] = right[:128, :]
    group_ref[128:256, :] = left[512:, :]
    group_ref[256:, :] = ahead[:128, :]


def norm_kernel(order_ref, x_ref, gain_ref, o_ref):
    states = x_ref[...].astype(jnp.float32)
    width = states.shape[1]
    scale = lax.rsqrt(jnp.sum(states * states, axis=1, keepdims=True) * (1.0 / width) + 1e-06)
    for k in range(width // 128):
        start = pl.multiple_of(order_ref[k] * 128, 128)
        part = x_ref[:, pl.ds(start, 128)].astype(jnp.float32)
        gain = gain_ref[:, pl.ds(start, 128)].astype(jnp.float32)
        o_ref[:, k * 128 : (k + 1) * 128] = (part * scale * gain).astype(jnp.bfloat16)


def normalise(order, states, gain):
    width = states.shape[1]
    steps = TILE // UNIT
    return pl.pallas_call(
        norm_kernel,
        out_shape=jax.ShapeDtypeStruct((TILE, width), jnp.bfloat16),
        grid_spec=pltpu.PrefetchScalarGridSpec(
            num_scalar_prefetch=1,
            grid=(steps,),
            in_specs=[
                pl.BlockSpec((UNIT, width), lambda i, order: (order[32] * steps + i, 0)),
                pl.BlockSpec((1, width), lambda i, order: (0, 0)),
            ],
            out_specs=pl.BlockSpec((UNIT, width), lambda i, order: (i, 0)),
        ),
        compiler_params=pltpu.CompilerParams(vmem_limit_bytes=VMEM_LIMIT),
        cost_estimate=pl.CostEstimate(
            flops=6 * TILE * width, bytes_accessed=4 * TILE * width, transcendentals=TILE
        ),
    )(order, states, gain)


def key_part(array, first, dy, start, count):
    return (array, first, count, ((dy * 1024 + start, count),))


def value_part(array, first, j, rows=512, i0=0):
    return (array, first, rows, tuple(((i0 + i) * 1024 + j * 128, 128) for i in range(rows // 128)))


def pick(x, columns):
    pieces = [x[:, at : at + count] for at, count in columns]
    return pieces[0] if len(pieces) == 1 else jnp.concatenate(pieces, axis=1)


def columns_of(parts):
    return [c for part in parts for c in part[3]]


def project_kernel(plan, *refs):
    n_tiles, n_in, key_parts, value_parts, depths, spans, keep = plan
    refs = list(refs)
    take = lambda n: [refs.pop(0) for _ in range(n)]
    tokens, key_src, value_src = take(n_tiles), take(len(key_parts)), take(len(value_parts))
    acc_in = take(2) if n_in else None
    outs = take(2)
    rest_out = refs.pop(0) if keep else None
    x_buf, in_buf, out_buf, key_w, value_w, x_sem, in_sem, w_sem, out_sem = refs

    def x_copies(i):
        ranges = [pl.ds(at, count) for at, count in spans[i]]
        return [
            pltpu.make_async_copy(tokens[i].at[:, r], x_buf.at[i % 2, :, r], x_sem.at[i, j])
            for j, r in enumerate(ranges)
        ]

    def in_copy(i, s):
        rows = pl.ds(i * TILE, TILE)
        return pltpu.make_async_copy(acc_in[s].at[rows], in_buf.at[i % 2, s], in_sem.at[i, s])

    def out_copy(i, s):
        rows = pl.ds(i * TILE, TILE)
        return pltpu.make_async_copy(out_buf.at[i % 2, s], outs[s].at[rows], out_sem.at[i, s])

    def load(i):
        for copy in x_copies(i):
            copy.start()
        if i < n_in:
            in_copy(i, 0).start()
            in_copy(i, 1).start()

    w_copies = [[], []]
    load(0)
    for s, (parts, srcs, place) in enumerate(
        ((key_parts, key_src, key_w), (value_parts, value_src, value_w))
    ):
        at = 0
        for j, (first, count, _) in enumerate(parts):
            src = srcs[j].at[pl.ds(first, count)]
            w_copies[s].append(
                pltpu.make_async_copy(src, place.at[pl.ds(at, count)], w_sem.at[s, j])
            )
            w_copies[s][-1].start()
            at += count
    ready = [0, 0]
    for i in range(n_tiles):
        if i + 1 < n_tiles:
            load(i + 1)
        for copy in x_copies(i):
            copy.wait()
        x = x_buf.at[i % 2]
        for s, (parts, place) in enumerate(((key_parts, key_w), (value_parts, value_w))):
            for copy in w_copies[s][ready[s] : depths[i][s]]:
                copy.wait()
            ready[s] = max(ready[s], depths[i][s])
            if i >= 2:
                out_copy(i - 2, s).wait()
            columns = [c for part in parts[: depths[i][s]] for c in part[2]]
            depth = sum(part[1] for part in parts[: depths[i][s]])
            total = jnp.dot(pick(x, columns), place[:depth, :], preferred_element_type=jnp.float32)
            if i < n_in:
                in_copy(i, s).wait()
                total = total + in_buf[i % 2, s]
            out_buf[i % 2, s] = total
            out_copy(i, s).start()
        if keep:
            rest_out[i * TILE : (i + 1) * TILE, :] = pick(x, keep)
    for i in range(max(0, n_tiles - 2), n_tiles):
        out_copy(i, 0).wait()
        out_copy(i, 1).wait()


def project(tokens, acc, key_parts, value_parts, depths, spans, keep=()):
    n_tiles, cols = len(tokens), 512
    rows, width = n_tiles * TILE, tokens[0].shape[1]
    n_in = acc[0].shape[0] // TILE if acc else 0
    strip = lambda parts: tuple(part[1:] for part in parts)
    plan = (n_tiles, n_in, strip(key_parts), strip(value_parts), depths, spans, tuple(keep))
    key_rows = sum(part[2] for part in key_parts)
    value_rows = sum(part[2] for part in value_parts)
    operands = list(tokens) + [part[0] for part in key_parts] + [part[0] for part in value_parts]
    operands += list(acc) if acc else []
    whole = pl.BlockSpec(memory_space=pl.ANY)
    shapes = [jax.ShapeDtypeStruct((rows, cols), jnp.float32)] * 2
    specs = [whole, whole]
    kept = sum(count for _, count in keep)
    if keep:
        shapes.append(jax.ShapeDtypeStruct((rows, kept), jnp.bfloat16))
        specs.append(pl.BlockSpec(memory_space=pltpu.VMEM))
    flops = 0
    for depth in depths:
        flops += 2 * TILE * cols * sum(part[2] for part in key_parts[: depth[0]])
        flops += 2 * TILE * cols * sum(part[2] for part in value_parts[: depth[1]])
    n_parts = max(len(key_parts), len(value_parts))
    return pl.pallas_call(
        functools.partial(project_kernel, plan),
        out_shape=tuple(shapes),
        in_specs=[whole] * len(operands),
        out_specs=tuple(specs),
        scratch_shapes=[
            pltpu.VMEM((2, TILE, width), jnp.bfloat16),
            pltpu.VMEM((2, 2, TILE, cols), jnp.float32),
            pltpu.VMEM((2, 2, TILE, cols), jnp.float32),
            pltpu.VMEM((key_rows, cols), jnp.bfloat16),
            pltpu.VMEM((value_rows, cols), jnp.bfloat16),
            pltpu.SemaphoreType.DMA((n_tiles, 4)),
            pltpu.SemaphoreType.DMA((n_tiles, 2)),
            pltpu.SemaphoreType.DMA((2, n_parts)),
            pltpu.SemaphoreType.DMA((n_tiles, 2)),
        ],
        compiler_params=pltpu.CompilerParams(vmem_limit_bytes=VMEM_LIMIT),
        cost_estimate=pl.CostEstimate(
            flops=flops,
            bytes_accessed=rows * width * 2 + (key_rows + value_rows) * cols * 2 + rows * cols * 8,
            transcendentals=0,
        ),
    )(*operands)


def attend_kernel(
    core_ref,
    own_facts,
    low_facts,
    high_facts,
    key_acc,
    value_acc,
    rest_ref,
    wk_ref,
    wv0,
    wv1,
    q_ref,
    o_ref,
    num,
    top,
    tot,
):
    step = pl.program_id(0)

    @pl.when(step == 0)
    def _():
        num[...] = jnp.zeros_like(num)
        tot[...] = jnp.zeros_like(tot)
        top[...] = jnp.full_like(top, FLOOR)

    def dot(a, b):
        return jnp.dot(a, b, preferred_element_type=jnp.float32)

    upper = jnp.where(step % 2 == 0, core_ref[0], 1 - core_ref[0])
    local = core_ref[1]

    def fact(p, field):
        at = 3 * field + p
        away = jnp.where(upper == 0, low_facts[0, at], high_facts[0, at])
        return jnp.where(step < 2, own_facts[0, at], away)

    slot = lax.broadcasted_iota(jnp.int32, (UNIT, 256), 0)
    question = lax.broadcasted_iota(jnp.int32, (UNIT, 256), 1) % 128 // 64
    masks = []
    for (p0, at0), (p1, at1) in (((0, 0), (1, 128)), ((0, 128), (2, 0)), ((1, 0), (2, 128))):
        live = jnp.where(upper == 0, fact(p0, 0) - at0, fact(p1, 0) - at1)
        owner = jnp.where(upper == 0, fact(p0, 1), fact(p1, 1)) - local
        masks.append((slot < live) & (question == owner))
    allowed = jnp.concatenate(masks, axis=0)

    keys = key_acc[...] + dot(rest_ref[:, :384], wk_ref[...])
    keys = keys.astype(jnp.bfloat16)
    values = (
        value_acc[...] + dot(rest_ref[:, 384:640], wv0[...]) + dot(rest_ref[:, 640:], wv1[...])
    )
    values = values.astype(jnp.bfloat16)
    for pair in range(2):
        columns = slice(pair * 128, (pair + 1) * 128)
        scores = jnp.where(allowed, dot(keys[:, columns], q_ref[pair]), NEG)
        old = top[pair, 0:1, :]
        new = jnp.maximum(old, jnp.max(scores, axis=0, keepdims=True))
        fade = jnp.exp(old - new)
        weights = jnp.exp(scores - new)
        top[pair, 0:1, :] = new
        tot[pair, 0:1, :] = tot[pair, 0:1, :] * fade + jnp.sum(weights, axis=0, keepdims=True)
        added = lax.dot_general(
            values[:, columns],
            weights.astype(jnp.bfloat16),
            (((0,), (0,)), ((), ())),
            preferred_element_type=jnp.float32,
        )
        for h in range(2):
            lanes = slice(h * 128, (h + 1) * 128)
            head = 2 * pair + h
            num[head] = num[head] * fade[:, lanes] + added[h * HD : (h + 1) * HD, lanes]

    @pl.when(step == pl.num_programs(0) - 1)
    def _():
        for head in range(4):
            pair, lanes = head // 2, slice(head % 2 * 128, head % 2 * 128 + 128)
            o_ref[head, :HD, :] = num[head]
            o_ref[head, HD : HD + 1, :] = top[pair, 0:1, lanes]
            o_ref[head, HD + 1 : HD + 2, :] = tot[pair, 0:1, lanes]
            o_ref[head, HD + 2 :, :] = jnp.zeros((6, 128), jnp.float32)


def attend(part, scalars, key_acc, value_acc, rest, ends, query_blocks):
    rows = key_acc.shape[0]
    accs = pl.BlockSpec((TILE, 256), lambda i: (i, part))
    return pl.pallas_call(
        attend_kernel,
        out_shape=jax.ShapeDtypeStruct((4, 72, 128), jnp.float32),
        grid=(rows // TILE,),
        in_specs=[pl.BlockSpec(memory_space=pltpu.SMEM)] * 4
        + [accs, accs, pl.BlockSpec((TILE, rest.shape[1]), lambda i: (i, 0))]
        + [pl.BlockSpec((a.shape[0], 256), lambda i: (0, part)) for a in ends]
        + [pl.BlockSpec((2, 128, 256), lambda i: (part, 0, 0))],
        out_specs=pl.BlockSpec((4, 72, 128), lambda i: (0, 0, 0)),
        scratch_shapes=[
            pltpu.VMEM((4, HD, 128), jnp.float32),
            pltpu.VMEM((2, 8, 256), jnp.float32),
            pltpu.VMEM((2, 8, 256), jnp.float32),
        ],
        compiler_params=pltpu.CompilerParams(vmem_limit_bytes=VMEM_LIMIT),
        cost_estimate=pl.CostEstimate(
            flops=2 * rows * 256 * (896 + 1024),
            bytes_accessed=rows * 256 * 8 + rows * 896 * 2 + 896 * 512,
            transcendentals=rows * 512,
        ),
    )(*scalars, key_acc, value_acc, rest, *ends, query_blocks)


def combine_kernel(colour_ref, *refs):
    o_ref = refs[-1]

    def head_result(a, b, head):
        top_a, top_b = a[head, HD : HD + 1, :], b[head, HD : HD + 1, :]
        top = jnp.maximum(top_a, top_b)
        fade_a, fade_b = jnp.exp(top_a - top), jnp.exp(top_b - top)
        total = a[head, HD + 1 : HD + 2, :] * fade_a + b[head, HD + 1 : HD + 2, :] * fade_b
        return (a[head, :HD, :] * fade_a + b[head, :HD, :] * fade_b) / total

    for part in range(2):
        own, opposite, left, right = refs[4 * part : 4 * part + 4]
        for side, (a, b) in enumerate(((own, opposite), (left, right))):
            colour = colour_ref[0] if side == 0 else 1 - colour_ref[0]
            for pair in range(2):
                block = jnp.concatenate(
                    [head_result(a, b, 2 * pair), head_result(a, b, 2 * pair + 1)], axis=0
                )
                start = pl.multiple_of(colour * 512 + part * 256 + pair * 128, 128)
                o_ref[:, pl.ds(start, 128)] = block.T.astype(jnp.bfloat16)


def body(passages, norm_gain, w_key, w_value, queries, lengths, passage_question):
    enc, x, core = lax.axis_index("enc"), lax.axis_index("dec"), lax.axis_index("mdl")
    y, z = enc // NZ, enc % NZ
    colour = (x % 2).reshape(1)
    pass_local, slot_count, width = passages.shape
    token_count = pass_local * slot_count

    two = jax.ShapeDtypeStruct((32, 1024), jnp.bfloat16)
    mine, theirs = small_call(pick_kernel, (two, two), colour, w_key, w_value)
    ring = (mine, shift_x(theirs, -1), shift_x(mine, 2), shift_x(theirs, 1))
    two = jax.ShapeDtypeStruct((128, 512), jnp.bfloat16)
    key_rows, value_rows = small_call(place_kernel, (two, two), x.reshape(1), *ring)

    order = [(y + dy) % NY * NZ + (z + dz) % NZ for dy in DY for dz in DZ]
    flat, gain = passages.reshape(token_count, width), norm_gain.reshape(1, width)
    sent = normalise(jnp.stack(order + [core]).astype(jnp.int32), flat, gain)
    join = lax.optimization_barrier
    facts = jnp.concatenate([lengths, passage_question]).reshape(1, 6)
    low, high = shift_x(facts, 1), shift_x(facts, -1)
    scalars = (jnp.stack([core, enc * 2]).astype(jnp.int32), facts, low, high)
    key_rows, value_rows, sent, scalars = join((key_rows, value_rows, sent, scalars))
    near = split_x(sent)
    kr1, kl1 = shift_z(key_rows, 1), shift_z(key_rows, -1)
    vy1, vy3 = shift_y(value_rows, 1), shift_y(value_rows, -1)
    kr1, kl1, vy1, vy3 = join((kr1, kl1, vy1, vy3))
    kr2, kl2 = shift_z(kr1, 1), shift_z(kl1, -1)
    vy2 = shift_y(value_rows, 2)
    kr2, kl2, vy2, flat, queries = join((kr2, kl2, vy2, flat, queries))
    right, left, group = small_call(
        gather_kernel,
        tuple(jax.ShapeDtypeStruct((640, 512), jnp.bfloat16) for _ in range(3)),
        None,
        key_rows, kr1, kl1, kr2, kl2, value_rows, vy1, vy3, vy2,
    )
    right1, left1 = shift_z(right, 1), shift_z(left, -1)
    group1, group3 = shift_y(group, 1), shift_y(group, -1)
    kept = normalise(jnp.stack(order + [1 - core]).astype(jnp.int32), flat, gain)
    rows_q = lax.dynamic_slice_in_dim(queries.reshape(128, -1), colour[0] * 512, 512, axis=1)
    turned = rows_q.T.reshape(4, 2, HD, 1, 128)
    eye = jnp.eye(2, dtype=jnp.bool_)[None, :, None, :, None]
    blocks = jnp.where(eye, turned, jnp.zeros((), jnp.bfloat16)).reshape(4, 128, 256)
    near, right1, left1, group1, group3, group, kept, blocks = join(
        (near, right1, left1, group1, group3, group, kept, blocks)
    )
    right2, left2 = shift_z(right1, 1), shift_z(left1, -1)
    group2 = shift_y(group, 2)
    far = other_core(near)
    early = ((0, 640), (1024, 640), (2048, 640), (3072, 384))
    keys_old = [key_part(g, 0, dy, 0, 640) for g, dy in ((group, 0), (group1, 1), (group3, 2))]
    values_old = [value_part(left, 0, 0), value_part(right1, 128, 1), value_part(left1, 0, 2)]
    acc = project((sent, kept, near), None, keys_old, values_old, ((3, 3),) * 3, (early,) * 3)
    acc, right2, left2, group2, far = join((tuple(acc), right2, left2, group2, far))
    shape = jax.ShapeDtypeStruct((384, 512), jnp.bfloat16)
    tail = small_call(end_kernel, shape, None, right1, left1, right2)
    right3, left3 = shift_z(right2[128:], 1), shift_z(left2[:512], -1)
    tail1, tail3 = shift_y(tail, 1), shift_y(tail, -1)
    keys_new = [key_part(tail, 0, 0, 640, 384), key_part(group2, 0, 3, 0, 640)]
    values_new = [value_part(right2, 128, 3), value_part(left2, 0, 4)]
    acc = project(
        (sent, kept, near, far),
        acc,
        keys_new + keys_old,
        values_new + values_old,
        ((2, 2),) * 3 + ((5, 5),),
        (((384, 640), (1408, 256), (2432, 256), (3072, 640)),) * 3 + (((0, 4096),),),
    )
    acc, right3, left3, tail1, tail3, tail = join((tuple(acc), right3, left3, tail1, tail3, tail))
    value_a, value_b = shift_z(right3[:256], 1), shift_z(left3[256:], -1)
    key_end = shift_y(tail, 2)
    key_acc, value_acc, rest = project(
        (sent, kept, near, far),
        acc,
        [key_part(tail1, 0, 1, 640, 384), key_part(tail3, 0, 2, 640, 384)],
        [value_part(right3, 0, 5), value_part(left3, 0, 6)],
        ((2, 2),) * 4,
        (tuple((i * 1024 + 640, 384) for i in range(NY)),) * 4,
        keep=((3712, 384),) + tuple((i * 1024 + 896, 128) for i in range(NY)),
    )

    ends = (key_end, value_a, value_b)
    shares = []
    for part in range(2):
        own = attend(part, scalars, key_acc, value_acc, rest, ends, blocks)
        shares += [own, shift_x(own, 2), shift_x(own, 1), shift_x(own, -1)]
        if part == 0:
            own, key_acc = join((own, key_acc))
    shape = jax.ShapeDtypeStruct((128, 1024), jnp.bfloat16)
    result = small_call(combine_kernel, shape, colour, *shares)
    return result.reshape(2, 64, 1024)


def solution(mesh):
    return jax.shard_map(
        body,
        mesh=mesh,
        in_specs=(
            P(("enc", "dec"), None, None),
            P(),
            P(("enc", "dec"), "mdl"),
            P(("enc", "dec"), "mdl"),
            P("enc", None, "mdl"),
            P(("enc", "dec")),
            P(("enc", "dec")),
        ),
        out_specs=P("enc", None, "mdl"),
        check_vma=False,
    )
```

```python
import functools

import jax
import jax.numpy as jnp
from jax import lax
from jax.experimental import pallas as pl
from jax.experimental.pallas import tpu as pltpu
from jax.sharding import PartitionSpec as P

HD = 64
NY, NZ, NX, NC = 4, 8, 4, 2
ENC, X, CORE = 0, 1, 2
DY = (0, -1, 1, 2)
DZ = (0, -1, 1, -2, 2, -3, 3, 4)
VMEM_LIMIT = 48 * 1024 * 1024
SMALL_VMEM = 16 * 1024 * 1024
PROJECT_VMEM = 20 * 1024 * 1024
NEG = -1e30
FLOOR = -1e29
TILE = 384
UNIT = 128


def shift_z(value, step):
    pairs = [(y * NZ + z, y * NZ + (z + step) % NZ) for y in range(NY) for z in range(NZ)]
    return lax.ppermute(value, "enc", pairs)


def shift_y(value, step):
    pairs = [(y * NZ + z, (y + step) % NY * NZ + z) for y in range(NY) for z in range(NZ)]
    return lax.ppermute(value, "enc", pairs)


def shift_x(value, step):
    return lax.ppermute(value, "dec", [(x, (x + step) % NX) for x in range(NX)])


def split_x(value):
    pairs = [
        (x * NC + c, (x + (1 if c == 0 else -1)) % NX * NC + c) for x in range(NX) for c in range(NC)
    ]
    return lax.ppermute(value, ("dec", "mdl"), pairs)


def other_core(value):
    return lax.ppermute(value, "mdl", [(0, 1), (1, 0)])


def facts_row(lengths_ref, question_ref, enc):
    lane = lax.broadcasted_iota(jnp.int32, (16, 128), 1)
    row = jnp.zeros((16, 128), jnp.int32)
    for p in range(3):
        row = jnp.where(lane == p, lengths_ref[p], row)
        row = jnp.where(lane == 3 + p, question_ref[p] - 2 * enc, row)
    return row.astype(jnp.float32)


def pick_kernel(ids, lengths_ref, question_ref, key_ref, value_ref, *refs):
    mine_ref, theirs_ref, lengths, question, sems = refs
    copies = [
        pltpu.make_async_copy(lengths_ref, lengths, sems.at[0]),
        pltpu.make_async_copy(question_ref, question, sems.at[1]),
    ]
    mine = pl.ds(pl.multiple_of(ids[X] % 2 * 512, 512), 512)
    theirs = pl.ds(pl.multiple_of((1 - ids[X] % 2) * 512, 512), 512)
    rows = pl.ds(0, 32)
    for i, (out, at) in enumerate(((mine_ref, mine), (theirs_ref, theirs))):
        for j, ref in enumerate((key_ref, value_ref)):
            place = out.at[rows, pl.ds(j * 512, 512)]
            copies.append(pltpu.make_async_copy(ref.at[:, at], place, sems.at[2 + 2 * i + j]))
    for copy in copies:
        copy.start()
    for copy in copies:
        copy.wait()
    theirs_ref[32:, :] = jnp.zeros((16, 1024), jnp.bfloat16)
    theirs_ref[32:, :128] = facts_row(lengths, question, ids[ENC]).astype(jnp.bfloat16)


def pick_columns(ids, lengths, questions, w_key, w_value):
    whole = pl.BlockSpec(memory_space=pltpu.HBM)
    return pl.pallas_call(
        pick_kernel,
        out_shape=(
            jax.ShapeDtypeStruct((32, 1024), jnp.bfloat16),
            jax.ShapeDtypeStruct((48, 1024), jnp.bfloat16),
        ),
        in_specs=[pl.BlockSpec(memory_space=pltpu.SMEM)] + [whole] * 4,
        out_specs=(pl.BlockSpec(memory_space=pltpu.VMEM),) * 2,
        scratch_shapes=[
            pltpu.SMEM((3,), jnp.int32),
            pltpu.SMEM((3,), jnp.int32),
            pltpu.SemaphoreType.DMA((6,)),
        ],
        compiler_params=pltpu.CompilerParams(vmem_limit_bytes=VMEM_LIMIT),
        cost_estimate=pl.CostEstimate(flops=0, bytes_accessed=1 << 19, transcendentals=0),
    )(ids, lengths, questions, w_key, w_value)


def place_kernel(ids, lengths_ref, question_ref, *refs):
    parts, (key_out, value_out, facts_out) = refs[:4], refs[4:]
    for j, part in enumerate(parts):
        at = pl.ds(pl.multiple_of((ids[X] + j) % NX * 32, 32), 32)
        key_out[at, :] = part[:32, :512]
        value_out[at, :] = part[:32, 512:]
    facts_out[0] = facts_row(lengths_ref, question_ref, ids[ENC])
    facts_out[1] = parts[3][32:, :128].astype(jnp.float32)
    facts_out[2] = parts[1][32:, :128].astype(jnp.float32)


def whole_block(a):
    return pl.BlockSpec(a.shape, lambda i: (0,) * len(a.shape))


def small_call(kernel, out_shape, scalars, *arrays):
    specs = [pl.BlockSpec(memory_space=pltpu.SMEM)] * len(scalars)
    specs += [whole_block(a) for a in arrays]
    return pl.pallas_call(
        kernel,
        out_shape=out_shape,
        grid=(1,),
        in_specs=specs,
        out_specs=jax.tree.map(whole_block, out_shape),
        compiler_params=pltpu.CompilerParams(vmem_limit_bytes=SMALL_VMEM),
        cost_estimate=pl.CostEstimate(
            flops=0, bytes_accessed=4 * sum(a.size for a in arrays), transcendentals=0
        ),
    )(*scalars, *arrays)


def gather_kernel(k0, kr1, kl1, kr2, kl2, v0, vy1, vy3, vy2, right_ref, left_ref, group_ref):
    for j, ref in enumerate((kr2, v0, vy1, vy3, vy2)):
        right_ref[j * 128 : (j + 1) * 128, :] = ref[...]
    for j, ref in enumerate((v0, vy1, vy3, vy2, kl2)):
        left_ref[j * 128 : (j + 1) * 128, :] = ref[...]
    for j, ref in enumerate((k0, kr1, kl1, kr2, kl2)):
        group_ref[j * 128 : (j + 1) * 128, :] = ref[...]


def end_kernel(right, left, ahead, group_ref):
    group_ref[:128, :] = right[:128, :]
    group_ref[128:256, :] = left[512:, :]
    group_ref[256:, :] = ahead[:128, :]


def norm_kernel(ids, x_ref, gain_ref, o_ref):
    states = x_ref[...].astype(jnp.float32)
    width = states.shape[1]
    y, z = ids[ENC] // NZ, ids[ENC] % NZ
    scale = lax.rsqrt(jnp.sum(states * states, axis=1, keepdims=True) * (1.0 / width) + 1e-06)
    for k in range(width // 128):
        block = (y + DY[k // NZ] + NY) % NY * NZ + (z + DZ[k % NZ] + NZ) % NZ
        start = pl.multiple_of(block * 128, 128)
        part = x_ref[:, pl.ds(start, 128)].astype(jnp.float32)
        gain = gain_ref[:, pl.ds(start, 128)].astype(jnp.float32)
        o_ref[:, k * 128 : (k + 1) * 128] = (part * scale * gain).astype(jnp.bfloat16)


def normalise(ids, other, states, gain):
    width, rows = states.shape[1], 128
    steps = TILE // rows
    half = lambda ids: 1 - ids[CORE] if other else ids[CORE]
    return pl.pallas_call(
        norm_kernel,
        out_shape=jax.ShapeDtypeStruct((TILE, width), jnp.bfloat16),
        grid_spec=pltpu.PrefetchScalarGridSpec(
            num_scalar_prefetch=1,
            grid=(steps,),
            in_specs=[
                pl.BlockSpec((rows, width), lambda i, ids: (half(ids) * steps + i, 0)),
                pl.BlockSpec((1, width), lambda i, ids: (0, 0)),
            ],
            out_specs=pl.BlockSpec((rows, width), lambda i, ids: (i, 0)),
        ),
        compiler_params=pltpu.CompilerParams(vmem_limit_bytes=VMEM_LIMIT),
        cost_estimate=pl.CostEstimate(
            flops=6 * TILE * width, bytes_accessed=4 * TILE * width, transcendentals=TILE
        ),
    )(ids, states, gain)


def key_part(array, first, dy, start, count):
    return (array, first, count, ((dy * 1024 + start, count),))


def value_part(array, first, j, rows=512, i0=0):
    return (array, first, rows, tuple(((i0 + i) * 1024 + j * 128, 128) for i in range(rows // 128)))


def pick(x, columns):
    pieces = [x[:, at : at + count] for at, count in columns]
    return pieces[0] if len(pieces) == 1 else jnp.concatenate(pieces, axis=1)


def columns_of(parts):
    return [c for part in parts for c in part[3]]


def project_kernel(plan, *refs):
    first, n_tiles, has_acc, add, key_parts, value_parts, spans, keep = plan
    refs = list(refs)
    take = lambda n: [refs.pop(0) for _ in range(n)]
    tokens, key_src, value_src = take(n_tiles), take(len(key_parts)), take(len(value_parts))
    acc_in = take(2) if has_acc else None
    outs = take(2)
    rest_out = refs.pop(0) if keep else None
    x_buf, in_buf, out_buf, key_w, value_w, x_sem, in_sem, w_sem, out_sem = refs

    def x_copies(i):
        ranges = [pl.ds(at, count) for at, count in spans]
        return [
            pltpu.make_async_copy(tokens[i].at[:, r], x_buf.at[i % 2, :, r], x_sem.at[i, j])
            for j, r in enumerate(ranges)
        ]

    def in_copy(i, s):
        rows = pl.ds((first + i) * TILE, TILE)
        return pltpu.make_async_copy(acc_in[s].at[rows], in_buf.at[i % 2, s], in_sem.at[i, s])

    def out_copy(i, s):
        rows = pl.ds((first + i) * TILE, TILE)
        return pltpu.make_async_copy(out_buf.at[i % 2, s], outs[s].at[rows], out_sem.at[i, s])

    def load(i):
        for copy in x_copies(i):
            copy.start()
        if add:
            in_copy(i, 0).start()
            in_copy(i, 1).start()

    w_copies = [[], []]
    load(0)
    for s, (parts, srcs, place) in enumerate(
        ((key_parts, key_src, key_w), (value_parts, value_src, value_w))
    ):
        at = 0
        for j, (row, count, _) in enumerate(parts):
            src = srcs[j].at[pl.ds(row, count)]
            w_copies[s].append(
                pltpu.make_async_copy(src, place.at[pl.ds(at, count)], w_sem.at[s, j])
            )
            w_copies[s][-1].start()
            at += count
    for i in range(n_tiles):
        if i + 1 < n_tiles:
            load(i + 1)
        for copy in x_copies(i):
            copy.wait()
        x = x_buf.at[i % 2]
        for s, (parts, place) in enumerate(((key_parts, key_w), (value_parts, value_w))):
            if i == 0:
                for copy in w_copies[s]:
                    copy.wait()
            if i >= 2:
                out_copy(i - 2, s).wait()
            columns = [c for part in parts for c in part[2]]
            total = jnp.dot(pick(x, columns), place[...], preferred_element_type=jnp.float32)
            if add:
                in_copy(i, s).wait()
                total = total + in_buf[i % 2, s]
            out_buf[i % 2, s] = total
            out_copy(i, s).start()
        if keep:
            rest_out[i * TILE : (i + 1) * TILE, :] = pick(x, keep)
    for i in range(max(0, n_tiles - 2), n_tiles):
        out_copy(i, 0).wait()
        out_copy(i, 1).wait()


def project(tokens, acc, add, key_parts, value_parts, spans, first=0, keep=()):
    n_tiles, cols = len(tokens), 512
    rows, width = 4 * TILE, tokens[0].shape[1]
    strip = lambda parts: tuple(part[1:] for part in parts)
    plan = (first, n_tiles, bool(acc), add, strip(key_parts), strip(value_parts), spans, keep)
    key_rows = sum(part[2] for part in key_parts)
    value_rows = sum(part[2] for part in value_parts)
    operands = list(tokens) + [part[0] for part in key_parts] + [part[0] for part in value_parts]
    aliases = {len(operands): 0, len(operands) + 1: 1} if acc else {}
    operands += list(acc)
    whole = pl.BlockSpec(memory_space=pl.ANY)
    shapes = [jax.ShapeDtypeStruct((rows, cols), jnp.float32)] * 2
    specs = [whole, whole]
    kept = sum(count for _, count in keep)
    if keep:
        shapes.append(jax.ShapeDtypeStruct((rows, kept), jnp.bfloat16))
        specs.append(pl.BlockSpec(memory_space=pltpu.VMEM))
    loaded = sum(count for _, count in spans)
    work = n_tiles * TILE
    return pl.pallas_call(
        functools.partial(project_kernel, plan),
        out_shape=tuple(shapes),
        in_specs=[whole] * len(operands),
        out_specs=tuple(specs),
        input_output_aliases=aliases,
        scratch_shapes=[
            pltpu.VMEM((2, TILE, width), jnp.bfloat16),
            pltpu.VMEM((2, 2, TILE, cols), jnp.float32),
            pltpu.VMEM((2, 2, TILE, cols), jnp.float32),
            pltpu.VMEM((key_rows, cols), jnp.bfloat16),
            pltpu.VMEM((value_rows, cols), jnp.bfloat16),
            pltpu.SemaphoreType.DMA((n_tiles, 4)),
            pltpu.SemaphoreType.DMA((n_tiles, 2)),
            pltpu.SemaphoreType.DMA((2, max(len(key_parts), len(value_parts)))),
            pltpu.SemaphoreType.DMA((n_tiles, 2)),
        ],
        compiler_params=pltpu.CompilerParams(vmem_limit_bytes=PROJECT_VMEM),
        cost_estimate=pl.CostEstimate(
            flops=2 * work * cols * (key_rows + value_rows),
            bytes_accessed=work * loaded * 2 + (key_rows + value_rows) * cols * 2 + work * cols * 8,
            transcendentals=0,
        ),
    )(*operands)


def attend_kernel(
    ids, facts_ref, key_acc, value_acc, rest_ref, wk_ref, wv0, wv1, q_ref, o_ref, num, top, tot
):
    step = pl.program_id(0)

    @pl.when(step == 0)
    def _():
        num[...] = jnp.zeros_like(num)
        tot[...] = jnp.zeros_like(tot)
        top[...] = jnp.full_like(top, FLOOR)

    def dot(a, b):
        return jnp.dot(a, b, preferred_element_type=jnp.float32)

    upper = jnp.where(step % 2 == 0, ids[CORE], 1 - ids[CORE])
    facts = facts_ref[jnp.where(step < 2, 0, 1 + upper)]
    slot = lax.broadcasted_iota(jnp.int32, (UNIT, 256), 0).astype(jnp.float32)
    question = lax.broadcasted_iota(jnp.int32, (UNIT, 256), 1) % 128 // 64
    question = question.astype(jnp.float32)
    masks = []
    for (p0, at0), (p1, at1) in (((0, 0), (1, 128)), ((0, 128), (2, 0)), ((1, 0), (2, 128))):
        pick_p = lambda f: jnp.where(upper == 0, facts[0:1, f + p0 : f + p0 + 1], facts[0:1, f + p1 : f + p1 + 1])
        live = pick_p(0) - jnp.where(upper == 0, at0, at1).astype(jnp.float32)
        masks.append((slot < live) & (question == pick_p(3)))
    allowed = jnp.concatenate(masks, axis=0)

    keys = key_acc[...] + dot(rest_ref[:, :384], wk_ref[...])
    keys = keys.astype(jnp.bfloat16)
    values = (
        value_acc[...] + dot(rest_ref[:, 384:640], wv0[...]) + dot(rest_ref[:, 640:], wv1[...])
    )
    values = values.astype(jnp.bfloat16)
    columns = [slice(pair * 128, (pair + 1) * 128) for pair in range(4)]
    scores = [
        jnp.where(allowed, dot(keys[:, columns[pair]], q_ref[pair]), NEG) for pair in range(4)
    ]
    old = [top[pair, 0:1, :] for pair in range(4)]
    new = [
        jnp.maximum(old[pair], jnp.max(scores[pair], axis=0, keepdims=True)) for pair in range(4)
    ]
    weights = [jnp.exp(scores[pair] - new[pair]) for pair in range(4)]
    added = [
        lax.dot_general(
            values[:, columns[pair]],
            weights[pair].astype(jnp.bfloat16),
            (((0,), (0,)), ((), ())),
            preferred_element_type=jnp.float32,
        )
        for pair in range(4)
    ]
    for pair in range(4):
        fade = jnp.exp(old[pair] - new[pair])
        total = jnp.sum(weights[pair], axis=0, keepdims=True)
        top[pair, 0:1, :] = new[pair]
        tot[pair, 0:1, :] = tot[pair, 0:1, :] * fade + total
        for h in range(2):
            lanes = slice(h * 128, (h + 1) * 128)
            head = 2 * pair + h
            num[head] = num[head] * fade[:, lanes] + added[pair][h * HD : (h + 1) * HD, lanes]

    @pl.when(step == pl.num_programs(0) - 1)
    def _():
        for head in range(8):
            pair, lanes = head // 2, slice(head % 2 * 128, head % 2 * 128 + 128)
            o_ref[head, :HD, :] = num[head]
            o_ref[head, HD : HD + 1, :] = top[pair, 0:1, lanes]
            o_ref[head, HD + 1 : HD + 2, :] = tot[pair, 0:1, lanes]
            o_ref[head, HD + 2 :, :] = jnp.zeros((6, 128), jnp.float32)


def attend(ids, facts, key_acc, value_acc, rest, ends, query_blocks):
    rows, cols = key_acc.shape
    tiled = lambda a: pl.BlockSpec((TILE, a.shape[1]), lambda i: (i, 0))
    arrays = (key_acc, value_acc, rest)
    return pl.pallas_call(
        attend_kernel,
        out_shape=jax.ShapeDtypeStruct((8, 72, 128), jnp.float32),
        grid=(rows // TILE,),
        in_specs=[pl.BlockSpec(memory_space=pltpu.SMEM), whole_block(facts)]
        + [tiled(a) for a in arrays]
        + [whole_block(a) for a in ends]
        + [whole_block(query_blocks)],
        out_specs=pl.BlockSpec((8, 72, 128), lambda i: (0, 0, 0)),
        scratch_shapes=[
            pltpu.VMEM((8, HD, 128), jnp.float32),
            pltpu.VMEM((4, 8, 256), jnp.float32),
            pltpu.VMEM((4, 8, 256), jnp.float32),
        ],
        compiler_params=pltpu.CompilerParams(vmem_limit_bytes=PROJECT_VMEM),
        cost_estimate=pl.CostEstimate(
            flops=2 * rows * cols * (896 + 1024),
            bytes_accessed=rows * cols * 8 + rows * 896 * 2 + 896 * cols * 2,
            transcendentals=rows * 1024,
        ),
    )(ids, facts, *arrays, *ends, query_blocks)


def combine_kernel(ids, own, opposite, left, right, o_ref):
    def head_result(a, b, head):
        top_a, top_b = a[head, HD : HD + 1, :], b[head, HD : HD + 1, :]
        top = jnp.maximum(top_a, top_b)
        fade_a, fade_b = jnp.exp(top_a - top), jnp.exp(top_b - top)
        total = a[head, HD + 1 : HD + 2, :] * fade_a + b[head, HD + 1 : HD + 2, :] * fade_b
        return (a[head, :HD, :] * fade_a + b[head, :HD, :] * fade_b) / total

    for side, (a, b) in enumerate(((own, opposite), (left, right))):
        colour = ids[X] % 2 if side == 0 else 1 - ids[X] % 2
        for pair in range(4):
            block = jnp.concatenate(
                [head_result(a, b, 2 * pair), head_result(a, b, 2 * pair + 1)], axis=0
            )
            start = pl.multiple_of(colour * 512 + pair * 128, 128)
            o_ref[:, pl.ds(start, 128)] = block.T.astype(jnp.bfloat16)


def body(passages, norm_gain, w_key, w_value, queries, lengths, passage_question):
    enc, x, core = lax.axis_index("enc"), lax.axis_index("dec"), lax.axis_index("mdl")
    ids = jnp.stack([enc, x, core]).astype(jnp.int32)
    pass_local, slot_count, width = passages.shape
    token_count = pass_local * slot_count

    shape = lambda rows, cols: jax.ShapeDtypeStruct((rows, cols), jnp.bfloat16)
    scalars = (ids, lengths, passage_question)
    mine, theirs = pick_columns(ids, lengths, passage_question, w_key, w_value)
    ring = (mine, shift_x(theirs, -1), shift_x(mine, 2), shift_x(theirs, 1))
    shapes = (shape(128, 512), shape(128, 512), jax.ShapeDtypeStruct((3, 16, 128), jnp.float32))
    key_rows, value_rows, facts = small_call(place_kernel, shapes, scalars, *ring)

    flat, gain = passages.reshape(token_count, width), norm_gain.reshape(1, width)
    sent = normalise(ids, False, flat, gain)
    join = lax.optimization_barrier
    key_rows, value_rows, sent = join((key_rows, value_rows, sent))
    near = split_x(sent)
    kr1, kl1 = shift_z(key_rows, 1), shift_z(key_rows, -1)
    vy1, vy3 = shift_y(value_rows, 1), shift_y(value_rows, -1)
    kr2, kl2 = shift_z(kr1, 1), shift_z(kl1, -1)
    vy2 = shift_y(value_rows, 2)
    kr2, kl2, vy1, vy3, vy2, flat, queries = join((kr2, kl2, vy1, vy3, vy2, flat, queries))
    right, left, group = small_call(
        gather_kernel,
        (shape(640, 512),) * 3,
        (),
        key_rows, kr1, kl1, kr2, kl2, value_rows, vy1, vy3, vy2,
    )
    right1, left1 = shift_z(right, 1), shift_z(left, -1)
    group1, group3 = shift_y(group, 1), shift_y(group, -1)
    kept = normalise(ids, True, flat, gain)
    rows_q = lax.dynamic_slice_in_dim(queries.reshape(128, -1), x % 2 * 512, 512, axis=1)
    turned = rows_q.T.reshape(4, 2, HD, 1, 128)
    eye = jnp.eye(2, dtype=jnp.bool_)[None, :, None, :, None]
    blocks = jnp.where(eye, turned, jnp.zeros((), jnp.bfloat16)).reshape(4, 128, 256)
    near, right1, left1, group1, group3, group, kept, blocks = join(
        (near, right1, left1, group1, group3, group, kept, blocks)
    )
    right2, left2 = shift_z(right1, 1), shift_z(left1, -1)
    group2 = shift_y(group, 2)
    far = other_core(near)
    early = ((0, 640), (1024, 640), (2048, 640), (3072, 384))
    keys_old = [key_part(g, 0, dy, 0, 640) for g, dy in ((group, 0), (group1, 1), (group3, 2))]
    values_old = [value_part(left, 0, 0), value_part(right1, 128, 1), value_part(left1, 0, 2)]
    acc = project((sent, kept, near), (), False, keys_old, values_old, early)
    acc = project((far,), acc, False, keys_old, values_old, early, first=3)
    acc, right2, left2, group2, far = join((tuple(acc), right2, left2, group2, far))
    tail = small_call(end_kernel, shape(384, 512), (), right1, left1, right2)
    right3, left3 = shift_z(right2[128:], 1), shift_z(left2[:512], -1)
    tail1, tail3 = shift_y(tail, 1), shift_y(tail, -1)
    keys_new = [key_part(tail, 0, 0, 640, 384), key_part(group2, 0, 3, 0, 640)]
    values_new = [value_part(right2, 128, 3), value_part(left2, 0, 4)]
    acc = project(
        (sent, kept, near, far),
        acc,
        True,
        keys_new,
        values_new,
        ((384, 640), (1408, 256), (2432, 256), (3072, 640)),
    )
    acc, right3, left3, tail1, tail3, tail = join((tuple(acc), right3, left3, tail1, tail3, tail))
    value_a, value_b = shift_z(right3[:256], 1), shift_z(left3[256:], -1)
    key_end = shift_y(tail, 2)
    key_acc, value_acc, rest = project(
        (sent, kept, near, far),
        acc,
        True,
        [key_part(tail1, 0, 1, 640, 384), key_part(tail3, 0, 2, 640, 384)],
        [value_part(right3, 0, 5), value_part(left3, 0, 6)],
        tuple((i * 1024 + 640, 384) for i in range(NY)),
        keep=((3712, 384),) + tuple((i * 1024 + 896, 128) for i in range(NY)),
    )

    part = attend(ids, facts, key_acc, value_acc, rest, (key_end, value_a, value_b), blocks)
    others = (shift_x(part, 2), shift_x(part, 1), shift_x(part, -1))
    result = small_call(combine_kernel, shape(128, 1024), (ids,), part, *others)
    return result.reshape(2, 64, 1024)


def solution(mesh):
    return jax.shard_map(
        body,
        mesh=mesh,
        in_specs=(
            P(("enc", "dec"), None, None),
            P(),
            P(("enc", "dec"), "mdl"),
            P(("enc", "dec"), "mdl"),
            P("enc", None, "mdl"),
            P(("enc", "dec")),
            P(("enc", "dec")),
        ),
        out_specs=P("enc", None, "mdl"),
        check_vma=False,
    )
```

```python
import functools

import jax
import jax.numpy as jnp
from jax import lax
from jax.experimental import pallas as pl
from jax.experimental.pallas import tpu as pltpu
from jax.sharding import PartitionSpec as P

HD = 64
NY, NZ, NX, NC = 4, 8, 4, 2
ENC, X, CORE = 0, 1, 2
DY = (0, -1, 1, 2)
DZ = (0, -1, 1, -2, 2, -3, 3, 4)
VMEM_LIMIT = 48 * 1024 * 1024
SMALL_VMEM = 16 * 1024 * 1024
PROJECT_VMEM = 16 * 1024 * 1024
PICK_VMEM = 63 * 1024 * 1024
NEG = -1e30
FLOOR = -1e29
TILE = 384
UNIT = 128


def shift_z(value, step):
    pairs = [(y * NZ + z, y * NZ + (z + step) % NZ) for y in range(NY) for z in range(NZ)]
    return lax.ppermute(value, "enc", pairs)


def shift_y(value, step):
    pairs = [(y * NZ + z, (y + step) % NY * NZ + z) for y in range(NY) for z in range(NZ)]
    return lax.ppermute(value, "enc", pairs)


def shift_x(value, step):
    return lax.ppermute(value, "dec", [(x, (x + step) % NX) for x in range(NX)])


def split_x(value):
    pairs = [
        (x * NC + c, (x + (1 if c == 0 else -1)) % NX * NC + c) for x in range(NX) for c in range(NC)
    ]
    return lax.ppermute(value, ("dec", "mdl"), pairs)


def other_core(value):
    return lax.ppermute(value, "mdl", [(0, 1), (1, 0)])


def facts_row(lengths_ref, question_ref, enc):
    lane = lax.broadcasted_iota(jnp.int32, (16, 128), 1)
    row = jnp.zeros((16, 128), jnp.int32)
    for p in range(3):
        row = jnp.where(lane == p, lengths_ref[p], row)
        row = jnp.where(lane == 3 + p, question_ref[p] - 2 * enc, row)
    return row.astype(jnp.float32)


def pick_kernel(ids, lengths_ref, question_ref, key_ref, value_ref, *refs):
    mine_ref, theirs_ref, lengths, question, sems = refs
    copies = [
        pltpu.make_async_copy(lengths_ref, lengths, sems.at[0]),
        pltpu.make_async_copy(question_ref, question, sems.at[1]),
    ]
    mine = pl.ds(pl.multiple_of(ids[X] % 2 * 512, 512), 512)
    theirs = pl.ds(pl.multiple_of((1 - ids[X] % 2) * 512, 512), 512)
    rows = pl.ds(0, 32)
    for i, (out, at) in enumerate(((mine_ref, mine), (theirs_ref, theirs))):
        for j, ref in enumerate((key_ref, value_ref)):
            place = out.at[rows, pl.ds(j * 512, 512)]
            copies.append(pltpu.make_async_copy(ref.at[:, at], place, sems.at[2 + 2 * i + j]))
    for copy in copies:
        copy.start()
    for copy in copies:
        copy.wait()
    theirs_ref[32:, :] = jnp.zeros((16, 1024), jnp.bfloat16)
    theirs_ref[32:, :128] = facts_row(lengths, question, ids[ENC]).astype(jnp.bfloat16)


def pick_columns(ids, lengths, questions, w_key, w_value):
    whole = pl.BlockSpec(memory_space=pl.ANY)
    return pl.pallas_call(
        pick_kernel,
        out_shape=(
            jax.ShapeDtypeStruct((32, 1024), jnp.bfloat16),
            jax.ShapeDtypeStruct((48, 1024), jnp.bfloat16),
        ),
        in_specs=[pl.BlockSpec(memory_space=pltpu.SMEM)] + [whole] * 4,
        out_specs=(pl.BlockSpec(memory_space=pltpu.VMEM),) * 2,
        scratch_shapes=[
            pltpu.SMEM((3,), jnp.int32),
            pltpu.SMEM((3,), jnp.int32),
            pltpu.SemaphoreType.DMA((6,)),
        ],
        compiler_params=pltpu.CompilerParams(vmem_limit_bytes=PICK_VMEM),
        cost_estimate=pl.CostEstimate(flops=0, bytes_accessed=1 << 19, transcendentals=0),
    )(ids, lengths, questions, w_key, w_value)


def place_kernel(ids, lengths_ref, question_ref, *refs):
    parts, (key_out, value_out, facts_out) = refs[:4], refs[4:]
    for j, part in enumerate(parts):
        at = pl.ds(pl.multiple_of((ids[X] + j) % NX * 32, 32), 32)
        key_out[at, :] = part[:32, :512]
        value_out[at, :] = part[:32, 512:]
    facts_out[0] = facts_row(lengths_ref, question_ref, ids[ENC])
    facts_out[1] = parts[3][32:, :128].astype(jnp.float32)
    facts_out[2] = parts[1][32:, :128].astype(jnp.float32)


def whole_block(a):
    return pl.BlockSpec(a.shape, lambda i: (0,) * len(a.shape))


def small_call(kernel, out_shape, scalars, *arrays):
    specs = [pl.BlockSpec(memory_space=pltpu.SMEM)] * len(scalars)
    specs += [whole_block(a) for a in arrays]
    return pl.pallas_call(
        kernel,
        out_shape=out_shape,
        grid=(1,),
        in_specs=specs,
        out_specs=jax.tree.map(whole_block, out_shape),
        compiler_params=pltpu.CompilerParams(vmem_limit_bytes=SMALL_VMEM),
        cost_estimate=pl.CostEstimate(
            flops=0, bytes_accessed=4 * sum(a.size for a in arrays), transcendentals=0
        ),
    )(*scalars, *arrays)


def gather_kernel(k0, kr1, kl1, kr2, kl2, v0, vy1, vy3, vy2, right_ref, left_ref, group_ref):
    for j, ref in enumerate((kr2, v0, vy1, vy3, vy2)):
        right_ref[j * 128 : (j + 1) * 128, :] = ref[...]
    for j, ref in enumerate((v0, vy1, vy3, vy2, kl2)):
        left_ref[j * 128 : (j + 1) * 128, :] = ref[...]
    for j, ref in enumerate((k0, kr1, kl1, kr2, kl2)):
        group_ref[j * 128 : (j + 1) * 128, :] = ref[...]


def end_kernel(right, left, ahead, group_ref):
    group_ref[:128, :] = right[:128, :]
    group_ref[128:256, :] = left[512:, :]
    group_ref[256:, :] = ahead[:128, :]


def norm_kernel(ids, x_ref, gain_ref, o_ref):
    states = x_ref[...].astype(jnp.float32)
    width = states.shape[1]
    y, z = ids[ENC] // NZ, ids[ENC] % NZ
    scale = lax.rsqrt(jnp.sum(states * states, axis=1, keepdims=True) * (1.0 / width) + 1e-06)
    for k in range(width // 128):
        block = (y + DY[k // NZ] + NY) % NY * NZ + (z + DZ[k % NZ] + NZ) % NZ
        start = pl.multiple_of(block * 128, 128)
        part = x_ref[:, pl.ds(start, 128)].astype(jnp.float32)
        gain = gain_ref[:, pl.ds(start, 128)].astype(jnp.float32)
        o_ref[:, k * 128 : (k + 1) * 128] = (part * scale * gain).astype(jnp.bfloat16)


def normalise(ids, other, states, gain):
    width, rows = states.shape[1], 128
    steps = TILE // rows
    half = lambda ids: 1 - ids[CORE] if other else ids[CORE]
    return pl.pallas_call(
        norm_kernel,
        out_shape=jax.ShapeDtypeStruct((TILE, width), jnp.bfloat16),
        grid_spec=pltpu.PrefetchScalarGridSpec(
            num_scalar_prefetch=1,
            grid=(steps,),
            in_specs=[
                pl.BlockSpec((rows, width), lambda i, ids: (half(ids) * steps + i, 0)),
                pl.BlockSpec((1, width), lambda i, ids: (0, 0)),
            ],
            out_specs=pl.BlockSpec((rows, width), lambda i, ids: (i, 0)),
        ),
        compiler_params=pltpu.CompilerParams(vmem_limit_bytes=VMEM_LIMIT),
        cost_estimate=pl.CostEstimate(
            flops=6 * TILE * width, bytes_accessed=4 * TILE * width, transcendentals=TILE
        ),
    )(ids, states, gain)


def key_part(array, first, dy, start, count):
    return (array, first, count, ((dy * 1024 + start, count),))


def value_part(array, first, j, rows=512, i0=0):
    return (array, first, rows, tuple(((i0 + i) * 1024 + j * 128, 128) for i in range(rows // 128)))


def pick(x, columns):
    pieces = [x[:, at : at + count] for at, count in columns]
    return pieces[0] if len(pieces) == 1 else jnp.concatenate(pieces, axis=1)


def columns_of(parts):
    return [c for part in parts for c in part[3]]


def project_kernel(plan, *refs):
    first, n_tiles, has_acc, add, key_parts, value_parts, keep = plan
    refs = list(refs)
    take = lambda n: [refs.pop(0) for _ in range(n)]
    tokens, key_src, value_src = take(n_tiles), take(len(key_parts)), take(len(value_parts))
    acc_in = take(2) if has_acc else None
    outs = take(2)
    rest_out = refs.pop(0) if keep else None
    weights = refs
    for parts, srcs, place in ((key_parts, key_src, weights[0]), (value_parts, value_src, weights[1])):
        at = 0
        for (row, count, _), w_ref in zip(parts, srcs):
            place[at : at + count, :] = w_ref[row : row + count, :]
            at += count
    for i in range(n_tiles):
        x = tokens[i]
        rows = slice((first + i) * TILE, (first + i + 1) * TILE)
        for s, parts in enumerate((key_parts, value_parts)):
            columns = [c for part in parts for c in part[2]]
            total = jnp.dot(pick(x, columns), weights[s][...], preferred_element_type=jnp.float32)
            outs[s][rows, :] = acc_in[s][rows, :] + total if add else total
        if keep:
            rest_out[i * TILE : (i + 1) * TILE, :] = pick(x, keep)


def project(tokens, acc, add, key_parts, value_parts, first=0, keep=()):
    n_tiles, cols = len(tokens), 512
    rows = 4 * TILE
    strip = lambda parts: tuple(part[1:] for part in parts)
    plan = (first, n_tiles, bool(acc), add, strip(key_parts), strip(value_parts), keep)
    key_rows = sum(part[2] for part in key_parts)
    value_rows = sum(part[2] for part in value_parts)
    operands = list(tokens) + [part[0] for part in key_parts] + [part[0] for part in value_parts]
    aliases = {len(operands): 0, len(operands) + 1: 1} if acc else {}
    operands += list(acc)
    whole = pl.BlockSpec(memory_space=pltpu.VMEM)
    shapes = [jax.ShapeDtypeStruct((rows, cols), jnp.float32)] * 2
    if keep:
        kept = sum(count for _, count in keep)
        shapes.append(jax.ShapeDtypeStruct((rows, kept), jnp.bfloat16))
    work = n_tiles * TILE
    return pl.pallas_call(
        functools.partial(project_kernel, plan),
        out_shape=tuple(shapes),
        in_specs=[whole] * len(operands),
        out_specs=(whole,) * len(shapes),
        input_output_aliases=aliases,
        scratch_shapes=[
            pltpu.VMEM((key_rows, cols), jnp.bfloat16),
            pltpu.VMEM((value_rows, cols), jnp.bfloat16),
        ],
        compiler_params=pltpu.CompilerParams(vmem_limit_bytes=PROJECT_VMEM),
        cost_estimate=pl.CostEstimate(
            flops=2 * work * cols * (key_rows + value_rows),
            bytes_accessed=work * 4096 + (key_rows + value_rows) * cols * 2 + work * cols * 8,
            transcendentals=0,
        ),
    )(*operands)


def attend_kernel(
    ids, facts_ref, key_acc, value_acc, rest_ref, wk_ref, wv0, wv1, q_ref, o_ref, num, top, tot
):
    step = pl.program_id(0)

    @pl.when(step == 0)
    def _():
        num[...] = jnp.zeros_like(num)
        tot[...] = jnp.zeros_like(tot)
        top[...] = jnp.full_like(top, FLOOR)

    def dot(a, b):
        return jnp.dot(a, b, preferred_element_type=jnp.float32)

    upper = jnp.where(step % 2 == 0, ids[CORE], 1 - ids[CORE])
    facts = facts_ref[jnp.where(step < 2, 0, 1 + upper)]
    slot = lax.broadcasted_iota(jnp.int32, (UNIT, 256), 0).astype(jnp.float32)
    question = lax.broadcasted_iota(jnp.int32, (UNIT, 256), 1) % 128 // 64
    question = question.astype(jnp.float32)
    masks = []
    for (p0, at0), (p1, at1) in (((0, 0), (1, 128)), ((0, 128), (2, 0)), ((1, 0), (2, 128))):
        pick_p = lambda f: jnp.where(upper == 0, facts[0:1, f + p0 : f + p0 + 1], facts[0:1, f + p1 : f + p1 + 1])
        live = pick_p(0) - jnp.where(upper == 0, at0, at1).astype(jnp.float32)
        masks.append((slot < live) & (question == pick_p(3)))
    allowed = jnp.concatenate(masks, axis=0)

    rows = pl.ds(pl.multiple_of(step * TILE, TILE), TILE)
    keys = key_acc[rows, :] + dot(rest_ref[rows, :384], wk_ref[...])
    keys = keys.astype(jnp.bfloat16)
    values = value_acc[rows, :] + dot(rest_ref[rows, 384:640], wv0[...])
    values = values + dot(rest_ref[rows, 640:], wv1[...])
    values = values.astype(jnp.bfloat16)
    columns = [slice(pair * 128, (pair + 1) * 128) for pair in range(4)]
    scores = [
        jnp.where(allowed, dot(keys[:, columns[pair]], q_ref[pair]), NEG) for pair in range(4)
    ]
    old = [top[pair, 0:1, :] for pair in range(4)]
    new = [
        jnp.maximum(old[pair], jnp.max(scores[pair], axis=0, keepdims=True)) for pair in range(4)
    ]
    weights = [jnp.exp(scores[pair] - new[pair]) for pair in range(4)]
    added = [
        lax.dot_general(
            values[:, columns[pair]],
            weights[pair].astype(jnp.bfloat16),
            (((0,), (0,)), ((), ())),
            preferred_element_type=jnp.float32,
        )
        for pair in range(4)
    ]
    for pair in range(4):
        fade = jnp.exp(old[pair] - new[pair])
        total = jnp.sum(weights[pair], axis=0, keepdims=True)
        top[pair, 0:1, :] = new[pair]
        tot[pair, 0:1, :] = tot[pair, 0:1, :] * fade + total
        for h in range(2):
            lanes = slice(h * 128, (h + 1) * 128)
            head = 2 * pair + h
            num[head] = num[head] * fade[:, lanes] + added[pair][h * HD : (h + 1) * HD, lanes]

    @pl.when(step == pl.num_programs(0) - 1)
    def _():
        for head in range(8):
            pair, lanes = head // 2, slice(head % 2 * 128, head % 2 * 128 + 128)
            o_ref[head, :HD, :] = num[head]
            o_ref[head, HD : HD + 1, :] = top[pair, 0:1, lanes]
            o_ref[head, HD + 1 : HD + 2, :] = tot[pair, 0:1, lanes]
            o_ref[head, HD + 2 :, :] = jnp.zeros((6, 128), jnp.float32)


def attend(ids, facts, key_acc, value_acc, rest, ends, query_blocks):
    rows, cols = key_acc.shape
    arrays = (key_acc, value_acc, rest)
    return pl.pallas_call(
        attend_kernel,
        out_shape=jax.ShapeDtypeStruct((8, 72, 128), jnp.float32),
        grid=(rows // TILE,),
        in_specs=[pl.BlockSpec(memory_space=pltpu.SMEM)]
        + [pl.BlockSpec(memory_space=pltpu.VMEM)] * (2 + len(arrays) + len(ends)),
        out_specs=pl.BlockSpec((8, 72, 128), lambda i: (0, 0, 0)),
        scratch_shapes=[
            pltpu.VMEM((8, HD, 128), jnp.float32),
            pltpu.VMEM((4, 8, 256), jnp.float32),
            pltpu.VMEM((4, 8, 256), jnp.float32),
        ],
        compiler_params=pltpu.CompilerParams(vmem_limit_bytes=PROJECT_VMEM),
        cost_estimate=pl.CostEstimate(
            flops=2 * rows * cols * (896 + 1024),
            bytes_accessed=rows * cols * 8 + rows * 896 * 2 + 896 * cols * 2,
            transcendentals=rows * 1024,
        ),
    )(ids, facts, *arrays, *ends, query_blocks)


def combine_kernel(ids, own, opposite, left, right, o_ref):
    def head_result(a, b, head):
        top_a, top_b = a[head, HD : HD + 1, :], b[head, HD : HD + 1, :]
        top = jnp.maximum(top_a, top_b)
        fade_a, fade_b = jnp.exp(top_a - top), jnp.exp(top_b - top)
        total = a[head, HD + 1 : HD + 2, :] * fade_a + b[head, HD + 1 : HD + 2, :] * fade_b
        return (a[head, :HD, :] * fade_a + b[head, :HD, :] * fade_b) / total

    for side, (a, b) in enumerate(((own, opposite), (left, right))):
        colour = ids[X] % 2 if side == 0 else 1 - ids[X] % 2
        for pair in range(4):
            block = jnp.concatenate(
                [head_result(a, b, 2 * pair), head_result(a, b, 2 * pair + 1)], axis=0
            )
            start = pl.multiple_of(colour * 512 + pair * 128, 128)
            o_ref[:, pl.ds(start, 128)] = block.T.astype(jnp.bfloat16)


def body(passages, norm_gain, w_key, w_value, queries, lengths, passage_question):
    enc, x, core = lax.axis_index("enc"), lax.axis_index("dec"), lax.axis_index("mdl")
    ids = jnp.stack([enc, x, core]).astype(jnp.int32)
    pass_local, slot_count, width = passages.shape
    token_count = pass_local * slot_count

    shape = lambda rows, cols: jax.ShapeDtypeStruct((rows, cols), jnp.bfloat16)
    scalars = (ids, lengths, passage_question)
    mine, theirs = pick_columns(ids, lengths, passage_question, w_key, w_value)
    ring = (mine, shift_x(theirs, -1), shift_x(mine, 2), shift_x(theirs, 1))
    shapes = (shape(128, 512), shape(128, 512), jax.ShapeDtypeStruct((3, 16, 128), jnp.float32))
    key_rows, value_rows, facts = small_call(place_kernel, shapes, scalars, *ring)

    flat, gain = passages.reshape(token_count, width), norm_gain.reshape(1, width)
    sent = normalise(ids, False, flat, gain)
    join = lax.optimization_barrier
    key_rows, value_rows, sent = join((key_rows, value_rows, sent))
    near = split_x(sent)
    kr1, kl1 = shift_z(key_rows, 1), shift_z(key_rows, -1)
    vy1, vy3 = shift_y(value_rows, 1), shift_y(value_rows, -1)
    kr2, kl2 = shift_z(kr1, 1), shift_z(kl1, -1)
    vy2 = shift_y(value_rows, 2)
    kr2, kl2, vy1, vy3, vy2, flat, queries = join((kr2, kl2, vy1, vy3, vy2, flat, queries))
    right, left, group = small_call(
        gather_kernel,
        (shape(640, 512),) * 3,
        (),
        key_rows, kr1, kl1, kr2, kl2, value_rows, vy1, vy3, vy2,
    )
    right1, left1 = shift_z(right, 1), shift_z(left, -1)
    group1, group3 = shift_y(group, 1), shift_y(group, -1)
    kept = normalise(ids, True, flat, gain)
    rows_q = lax.dynamic_slice_in_dim(queries.reshape(128, -1), x % 2 * 512, 512, axis=1)
    turned = rows_q.T.reshape(4, 2, HD, 1, 128)
    eye = jnp.eye(2, dtype=jnp.bool_)[None, :, None, :, None]
    blocks = jnp.where(eye, turned, jnp.zeros((), jnp.bfloat16)).reshape(4, 128, 256)
    near, right1, left1, group1, group3, group, kept, blocks = join(
        (near, right1, left1, group1, group3, group, kept, blocks)
    )
    right2, left2 = shift_z(right1, 1), shift_z(left1, -1)
    group2 = shift_y(group, 2)
    far = other_core(near)
    keys_old = [key_part(g, 0, dy, 0, 640) for g, dy in ((group, 0), (group1, 1), (group3, 2))]
    values_old = [value_part(left, 0, 0), value_part(right1, 128, 1), value_part(left1, 0, 2)]
    acc = project((sent, kept, near), (), False, keys_old, values_old)
    acc = project((far,), acc, False, keys_old, values_old, first=3)
    acc, right2, left2 = join((tuple(acc), right2, left2))
    tail = small_call(end_kernel, shape(384, 512), (), right1, left1, right2)
    right3, left3 = shift_z(right2[128:], 1), shift_z(left2[:512], -1)
    tail1, tail3 = shift_y(tail, 1), shift_y(tail, -1)
    keys_new = [key_part(tail, 0, 0, 640, 384), key_part(group2, 0, 3, 0, 640)]
    values_new = [value_part(right2, 128, 3), value_part(left2, 0, 4)]
    acc = project(
        (sent, kept, near, far),
        acc,
        True,
        keys_new,
        values_new,
    )
    acc, right3, left3, tail1, tail3, tail = join((tuple(acc), right3, left3, tail1, tail3, tail))
    value_a, value_b = shift_z(right3[:256], 1), shift_z(left3[256:], -1)
    key_end = shift_y(tail, 2)
    key_acc, value_acc, rest = project(
        (sent, kept, near, far),
        acc,
        True,
        [key_part(tail1, 0, 1, 640, 384), key_part(tail3, 0, 2, 640, 384)],
        [value_part(right3, 0, 5), value_part(left3, 0, 6)],
        keep=((3712, 384),) + tuple((i * 1024 + 896, 128) for i in range(NY)),
    )

    part = attend(ids, facts, key_acc, value_acc, rest, (key_end, value_a, value_b), blocks)
    others = (shift_x(part, 2), shift_x(part, 1), shift_x(part, -1))
    result = small_call(combine_kernel, shape(128, 1024), (ids,), part, *others)
    return result.reshape(2, 64, 1024)


def solution(mesh):
    return jax.shard_map(
        body,
        mesh=mesh,
        in_specs=(
            P(("enc", "dec"), None, None),
            P(),
            P(("enc", "dec"), "mdl"),
            P(("enc", "dec"), "mdl"),
            P("enc", None, "mdl"),
            P(("enc", "dec")),
            P(("enc", "dec")),
        ),
        out_specs=P("enc", None, "mdl"),
        check_vma=False,
    )
```
